512 devices in a mesh: row: 16 (over y_lo, z), col: 32 (over y_hi, x, core).
Axes of the slice: x: 4, y: 8 (y_hi: 4, y_lo: 2; y = y_hi * 2 + y_lo), z: 8, core: 2. Of those that a mesh axis runs over, the one named last changes fastest.
Arguments:
- features: bfloat16 [131072, 128], P(('row', 'col')), may hold values from -16 to 16
- scales: bfloat16 [131072], P(('row', 'col')), may hold values from 0.29882812 to 3
- vectors: float32 [32, 131072], P(None, ('row', 'col')), may hold values from -4 to 4
- pattern: int32 [16, 32, 2, 128], P('row', 'col'), may hold values from 0 to 511, as said below
- counts: int32 [16, 32], P('row', 'col'), may hold values from 1 to 128
Outputs:
- product: float32 [32, 131072], P(None, ('row', 'col'))
The draws below stay inside these ranges and needn't reach their ends.
Inputs may be any that keep to these rules, and one draw needn't show every extreme that they name: For s < counts[r, c] the pairs (pattern[r, c, 0, s], pattern[r, c, 1, s]) = (i, j) are distinct, i <= j, i // 32 = r and j % 32 = c; slots s >= counts[r, c] hold block numbers that are to be ignored.
All inputs are finite; a program needn't handle non-finite values.
Results may differ from the reference program's by a relative error of at most 0.0041.
Values may be sent and summed in bfloat16 or wider, within the bound.
No kernel may reach another device: no remote copies, remote signals or barrier semaphores. Data moves between devices by JAX's collectives and lax.ppermute only.
A program may use at most 64 MiB of HBM per device.

```python
import math
import jax
import jax.numpy as jnp
from jax import lax

TILE = 256
DESC = 128
VECS = 32
SLOTS = 128
BLOCKS = 512
ROWS = 131072
N_ROW = 16
N_COL = 32


def tile_layout(key):
    count_key = jax.random.fold_in(key, 0)
    score_key = jax.random.fold_in(key, 2)
    grid_row = jnp.arange(N_ROW, dtype=jnp.int32)[:, None, None]
    grid_col = jnp.arange(N_COL, dtype=jnp.int32)[None, :, None]
    places = jnp.arange(BLOCKS, dtype=jnp.int32)[None, None, :]
    block_row = grid_row * N_COL + places // N_ROW + 0 * grid_col
    block_col = places % N_ROW * N_COL + grid_col + 0 * grid_row
    valid = (block_row <= block_col).astype(jnp.int32)
    avail = jnp.sum(valid, axis=-1)
    spread = SLOTS // 8
    remain = N_ROW - grid_row[:, :, 0]
    base = SLOTS * remain * remain // (N_ROW * N_ROW) + jax.random.randint(count_key, (N_ROW, N_COL), -spread, spread + 1)
    chosen_one = (grid_row[:, :, 0] == 0) & (grid_col[:, :, 0] == N_COL - 1)
    base = jnp.where(chosen_one, SLOTS, base)
    tile_count = jnp.clip(base, 1, jnp.minimum(avail, SLOTS)).astype(jnp.int32)
    noise = jax.random.randint(score_key, (N_ROW, N_COL, BLOCKS), 0, 1 << 20)
    favored = ((places == 0) | (block_col == BLOCKS - 1)).astype(jnp.int32)
    score = noise * BLOCKS + places + (1 - valid) * (1 << 30) - favored * (1 << 29)
    order = jnp.argsort(score, axis=-1, stable=True)
    picked = order[..., jnp.arange(SLOTS) % BLOCKS]
    rows_taken = jnp.take_along_axis(block_row, picked, axis=-1)
    cols_taken = jnp.take_along_axis(block_col, picked, axis=-1)
    pattern = jnp.stack([rows_taken, cols_taken], axis=2).astype(jnp.int32)
    return (pattern, tile_count)


def draw_pattern(key, part):
    pattern, tile_count = tile_layout(key)
    return pattern


def draw_counts(key, part):
    pattern, tile_count = tile_layout(key)
    return tile_count


def draw_features(key, part):
    key = jax.random.fold_in(key, 11)
    coord = jnp.arange(DESC, dtype=jnp.int32)
    amplitude = jnp.where(coord < DESC // 8, 3.5, 0.5).astype(jnp.float32)
    base = jnp.clip(jax.random.normal(key, (ROWS, DESC), jnp.float32), -4.5, 4.5)
    return (base * amplitude[None, :]).astype(jnp.bfloat16)


def level_of(key, shape, cuts, smallest, high):
    loudness, own = 1.0, jax.random.fold_in(key, 6)
    for axis_at, blocks in cuts:
        draws = jnp.exp(jax.random.uniform(jax.random.fold_in(own, axis_at), (blocks,), jnp.float32, smallest / len(cuts), high / len(cuts)))
        loudness = loudness * jnp.repeat(draws, shape[axis_at] // blocks).reshape([-1 if axis == axis_at else 1 for axis in range(len(shape))])
    return loudness


def bell_draw(key, extent, scale, limit, cuts=(), kind=jnp.bfloat16):
    factor_of = level_of(key, extent, cuts, -0.22, 0.18) if cuts else 1.0
    result = jax.random.normal(key, extent, jnp.float32) * scale * factor_of
    return jnp.minimum(jnp.maximum(result, -limit), limit).astype(kind)


def setup_inputs(seed: int = 0) -> dict:
    streams_of = jax.random.split(jax.random.key(seed), 6)
    return {
        "features": draw_features(jax.random.fold_in(streams_of[5], 71), 0),
        "scales": jnp.clip(jnp.exp(math.log(3.0) - 2.306499 * jax.random.uniform(streams_of[1], (ROWS,), jnp.float32) ** level_of(streams_of[1], (ROWS,), ((0, 512),), -0.2, 0.2)), 0.29882812, 3.0).astype(jnp.bfloat16),
        "vectors": bell_draw(streams_of[2], (VECS, ROWS), 0.5, 4.0, ((1, 512),), jnp.float32),
        "pattern": draw_pattern(jax.random.fold_in(streams_of[5], 71), 0),
        "counts": draw_counts(jax.random.fold_in(streams_of[5], 71), 0),
    }


def reference(features, scales, vectors, pattern, counts):
    narrow = vectors.astype(jnp.bfloat16).astype(jnp.float32)
    feat_wide = features.astype(jnp.float32)
    norm_all = jnp.sum(feat_wide * feat_wide, axis=1).reshape(BLOCKS, TILE)
    feat_blocks = feat_wide.reshape(BLOCKS, TILE, DESC)
    scale_blocks = scales.astype(jnp.float32).reshape(BLOCKS, TILE)
    vec_blocks = narrow.reshape(VECS, BLOCKS, TILE)
    slot_ids = jnp.arange(SLOTS, dtype=jnp.int32)

    def one_device(running, device_item):
        tile_pairs, tile_count = device_item
        block_rows = tile_pairs[0]
        block_cols = tile_pairs[1]
        live_slot = (slot_ids < tile_count).astype(jnp.float32)
        mirror_live = live_slot * (block_rows != block_cols).astype(jnp.float32)
        inner_dot = jnp.einsum("gpd,gqd->gpq", feat_blocks[block_rows], feat_blocks[block_cols], precision=lax.Precision.HIGHEST)
        exponent = (2.0 * inner_dot - norm_all[block_rows][:, :, None] - norm_all[block_cols][:, None, :]) / DESC
        tile_block = scale_blocks[block_rows][:, :, None] * scale_blocks[block_cols][:, None, :] * jnp.exp(exponent)
        tile_block = tile_block.astype(jnp.bfloat16).astype(jnp.float32)
        forward_part = jnp.einsum("gpq,kgq->gkp", tile_block, vec_blocks[:, block_cols], precision=lax.Precision.HIGHEST)
        mirror_part = jnp.einsum("gpq,kgp->gkq", tile_block, vec_blocks[:, block_rows], precision=lax.Precision.HIGHEST)
        running = running.at[block_rows].add(forward_part * live_slot[:, None, None])
        running = running.at[block_cols].add(mirror_part * mirror_live[:, None, None])
        return running, None

    start = jnp.zeros((BLOCKS, VECS, TILE), jnp.float32)
    items = (pattern.reshape(BLOCKS, 2, SLOTS), counts.reshape(BLOCKS))
    running, unused = lax.scan(one_device, start, items)
    return jnp.transpose(running, (1, 0, 2)).reshape(VECS, ROWS)
```

```python
import math

import jax
import jax.numpy as jnp
from jax import lax
from jax.experimental import pallas as pl
from jax.experimental.pallas import tpu as pltpu
from jax.sharding import PartitionSpec as P

TILE = 256
DESC = 128
VECS = 32
AUG = 16
DEPTH = DESC + AUG
PACK = DEPTH + VECS
UNROLL = 4

COL_SIZES = (4, 4, 2)
ROW_SIZES = (2, 8)
ROW_PARTS = 8
COL_PARTS = 1

POWER = math.log2(math.e) * 2.0 / DESC


def pack_kernel(feat_ref, scale_ref, vec_ref, row_ref, col_ref):
    turned = feat_ref[...].astype(jnp.float32).T
    norm = jnp.sum(turned * turned, axis=0, keepdims=True)
    offset = (DESC // 2) * jnp.log(scale_ref[...].astype(jnp.float32)) - 0.5 * norm
    high = offset.astype(jnp.bfloat16).astype(jnp.float32)
    rest = offset - high
    middle = rest.astype(jnp.bfloat16).astype(jnp.float32)
    low = (rest - middle).astype(jnp.bfloat16).astype(jnp.float32)
    place = lax.broadcasted_iota(jnp.int32, (AUG, TILE), 0)

    def offset_rows(first_own, first_one):
        own = place - first_own
        rows = jnp.where(own == 0, high, jnp.where(own == 1, middle, jnp.where(own == 2, low, 0.0)))
        one = place - first_one
        return jnp.where((one >= 0) & (one < 3), 1.0, rows).astype(jnp.bfloat16)

    descriptors = turned.astype(jnp.bfloat16)
    narrow = vec_ref[...].astype(jnp.bfloat16)
    for ref, rows in ((row_ref, offset_rows(0, 3)), (col_ref, offset_rows(3, 0))):
        ref[0:DESC, :] = descriptors
        ref[DESC:DEPTH, :] = rows
        ref[DEPTH:PACK, :] = narrow


def pack_blocks(features, scales, vectors):
    shape = jax.ShapeDtypeStruct((PACK, TILE), jnp.bfloat16)
    return pl.pallas_call(pack_kernel, out_shape=(shape, shape), name="pack_blocks")(
        features, scales.reshape(1, TILE), vectors
    )


def tiles_kernel(slots_ref, count_ref, *refs):
    rows_from, cols_from = refs[:ROW_PARTS], refs[ROW_PARTS : ROW_PARTS + COL_PARTS]
    forward_ref, mirror_ref = refs[ROW_PARTS + COL_PARTS : ROW_PARTS + COL_PARTS + 2]
    rows_ref, cols_ref, turned_ref, fsum_ref, msum_ref, row_sems, col_sems = refs[ROW_PARTS + COL_PARTS + 2 :]
    row_span = rows_ref.shape[0]
    col_span = cols_ref.shape[0]

    def copies(sources, target, sems):
        size = target.shape[0] // len(sources)
        return [
            pltpu.make_async_copy(source, target.at[pl.ds(at * size, size)], sems.at[at])
            for at, source in enumerate(sources)
        ]

    row_copies = copies(rows_from, rows_ref, row_sems)
    col_copies = copies(cols_from, cols_ref, col_sems)
    for copy in row_copies + col_copies:
        copy.start()

    fsum_ref[...] = jnp.zeros_like(fsum_ref)
    msum_ref[...] = jnp.zeros_like(msum_ref)

    part = row_span // ROW_PARTS
    for at, copy in enumerate(row_copies):
        copy.wait()

        @pl.loop(at * part, (at + 1) * part)
        def _(block):
            turned_ref[block] = rows_ref[block, 0:DEPTH, :].T

    for copy in col_copies:
        copy.wait()

    def tile(slot):
        row_at = slots_ref[0, slot]
        col_at = slots_ref[1, slot]
        score = jnp.dot(turned_ref[row_at], cols_ref[col_at, 0:DEPTH, :], preferred_element_type=jnp.float32)
        block = jnp.exp2(score * POWER).astype(jnp.bfloat16)
        forward = lax.dot_general(
            cols_ref[col_at, DEPTH:PACK, :], block, (((1,), (1,)), ((), ())), preferred_element_type=jnp.float32
        )
        mirror = jnp.dot(rows_ref[row_at, DEPTH:PACK, :], block, preferred_element_type=jnp.float32)
        return slots_ref[2, slot], slots_ref[3, slot], forward, mirror

    @pl.loop(0, lax.div(count_ref[0, 0] + (UNROLL - 1), UNROLL))
    def _(group):
        done = [tile(group * UNROLL + step) for step in range(UNROLL)]
        for forward_at, mirror_at, forward, mirror in done:
            fsum_ref[forward_at] += forward
            msum_ref[mirror_at] += mirror

    forward_ref[...] = fsum_ref[0:row_span].astype(jnp.bfloat16)
    mirror_ref[...] = msum_ref[0:col_span].astype(jnp.bfloat16)


def tile_products(slots, tile_count, row_parts, col_parts):
    row_span = sum(part.shape[0] for part in row_parts)
    col_span = sum(part.shape[0] for part in col_parts)
    smem = pl.BlockSpec(memory_space=pltpu.SMEM)
    vmem = pl.BlockSpec(memory_space=pltpu.VMEM)
    anywhere = pl.BlockSpec(memory_space=pl.ANY)
    return pl.pallas_call(
        tiles_kernel,
        out_shape=(
            jax.ShapeDtypeStruct((row_span, VECS, TILE), jnp.bfloat16),
            jax.ShapeDtypeStruct((col_span, VECS, TILE), jnp.bfloat16),
        ),
        in_specs=[smem, smem] + [anywhere] * (ROW_PARTS + COL_PARTS),
        out_specs=(vmem, vmem),
        scratch_shapes=[
            pltpu.VMEM((row_span, PACK, TILE), jnp.bfloat16),
            pltpu.VMEM((col_span, PACK, TILE), jnp.bfloat16),
            pltpu.VMEM((row_span, TILE, DEPTH), jnp.bfloat16),
            pltpu.VMEM((row_span + 1, VECS, TILE), jnp.float32),
            pltpu.VMEM((col_span + 1, VECS, TILE), jnp.float32),
            pltpu.SemaphoreType.DMA((ROW_PARTS,)),
            pltpu.SemaphoreType.DMA((COL_PARTS,)),
        ],
        compiler_params=pltpu.CompilerParams(vmem_limit_bytes=48 * 1024 * 1024),
        name="tile_products",
    )(slots, tile_count, *row_parts, *col_parts)


def shifted(value, axis, sizes, part, distance):
    pairs = []
    for source in range(math.prod(sizes)):
        place = list(split_index(source, sizes))
        place[part] = (place[part] + distance) % sizes[part]
        target = 0
        for at, size in zip(place, sizes):
            target = target * size + at
        pairs.append((source, target))
    return lax.ppermute(value, axis, pairs)


def split_index(index, sizes):
    place = []
    for size in reversed(sizes):
        place.append(index & (size - 1))
        index = index >> (size.bit_length() - 1)
    return tuple(reversed(place))


def gather_rows(own):
    along_y = jnp.stack([own] + [shifted(own, "col", COL_SIZES, 0, step) for step in range(1, 4)])
    parts = [along_y] + [shifted(along_y, "col", COL_SIZES, 1, step) for step in range(1, 4)]
    return parts + [shifted(part, "col", COL_SIZES, 2, 1) for part in parts]


def gather_cols(own):
    span = math.prod(ROW_SIZES)
    return [lax.all_to_all(jnp.broadcast_to(own, (span,) + own.shape), "row", 0, 0, tiled=True)]


def slot_places(tile_pairs, tile_count):
    row_span = math.prod(COL_SIZES)
    col_span = math.prod(ROW_SIZES)
    i, j = tile_pairs[0], tile_pairs[1]
    local_row, local_col = lax.rem(i, row_span), lax.div(j, row_span)

    here = split_index(lax.axis_index("col"), COL_SIZES)
    there = split_index(local_row, COL_SIZES)
    y_hi, x, core = [(mine - other) & (size - 1) for mine, other, size in zip(here, there, COL_SIZES)]
    live = jnp.arange(tile_pairs.shape[1], dtype=jnp.int32) < tile_count
    return jnp.stack(
        [
            (core * 4 + x) * 4 + y_hi,
            local_col,
            jnp.where(live, local_row, row_span),
            jnp.where(live & (i != j), local_col, col_span),
        ]
    )


def body(features, scales, vectors, pattern, counts):
    row_own, col_own = pack_blocks(features, scales, vectors)
    row_parts = gather_rows(row_own)
    col_parts = gather_cols(col_own)
    slots = slot_places(pattern[0, 0], counts[0, 0])
    forward, mirror = tile_products(slots, counts, row_parts, col_parts)
    forward = lax.all_to_all(forward, "col", 0, 0, tiled=True)
    mirror = lax.all_to_all(mirror, "row", 0, 0, tiled=True)
    return jnp.sum(forward.astype(jnp.float32), axis=0) + jnp.sum(mirror.astype(jnp.float32), axis=0)


def solution(mesh):
    placed = (
        P(("row", "col"), None),
        P(("row", "col")),
        P(None, ("row", "col")),
        P("row", "col", None, None),
        P("row", "col"),
    )
    return jax.shard_map(
        body, mesh=mesh, in_specs=placed, out_specs=P(None, ("row", "col")), check_vma=False
    )
```

```python
import math

import jax
import jax.numpy as jnp
from jax import lax
from jax.experimental import pallas as pl
from jax.experimental.pallas import tpu as pltpu
from jax.sharding import PartitionSpec as P

TILE = 256
DESC = 128
VECS = 32
AUG = 16
DEPTH = DESC + AUG
PACK = DEPTH + VECS
FULL = 256
UNROLL = 8

COL_SIZES = (4, 4, 2)
ROW_SIZES = (2, 8)
ROW_PARTS = 8
COL_PARTS = 1

POWER = math.log2(math.e) * 2.0 / DESC


def pack_kernel(feat_ref, scale_ref, vec_ref, row_ref, col_ref):
    turned = feat_ref[...].astype(jnp.float32).T
    norm = jnp.sum(turned * turned, axis=0, keepdims=True)
    offset = (DESC // 2) * jnp.log(scale_ref[...].astype(jnp.float32)) - 0.5 * norm
    high = offset.astype(jnp.bfloat16).astype(jnp.float32)
    rest = offset - high
    middle = rest.astype(jnp.bfloat16).astype(jnp.float32)
    low = (rest - middle).astype(jnp.bfloat16).astype(jnp.float32)
    place = lax.broadcasted_iota(jnp.int32, (AUG, TILE), 0)

    def offset_rows(first_own, first_one):
        own = place - first_own
        rows = jnp.where(own == 0, high, jnp.where(own == 1, middle, jnp.where(own == 2, low, 0.0)))
        one = place - first_one
        return jnp.where((one >= 0) & (one < 3), 1.0, rows).astype(jnp.bfloat16)

    descriptors = turned.astype(jnp.bfloat16)
    narrow = vec_ref[...].astype(jnp.bfloat16)
    for ref, rows in ((row_ref, offset_rows(0, 3)), (col_ref, offset_rows(3, 0))):
        ref[0:DESC, :] = descriptors
        ref[DESC:DEPTH, :] = rows
        ref[DEPTH:PACK, :] = narrow


def pack_blocks(features, scales, vectors):
    shape = jax.ShapeDtypeStruct((PACK, TILE), jnp.bfloat16)
    return pl.pallas_call(pack_kernel, out_shape=(shape, shape), name="pack_blocks")(
        features, scales.reshape(1, TILE), vectors
    )


def tiles_kernel(slots_ref, count_ref, *refs):
    rows_from, cols_from = refs[:ROW_PARTS], refs[ROW_PARTS : ROW_PARTS + COL_PARTS]
    forward_ref, other_ref, mirror_ref = refs[ROW_PARTS + COL_PARTS : ROW_PARTS + COL_PARTS + 3]
    rows_ref, cols_ref, turned_ref, fsum_ref, msum_ref, row_sems, col_sems = refs[ROW_PARTS + COL_PARTS + 3 :]
    row_span = rows_ref.shape[0]
    col_span = cols_ref.shape[0]

    cols_ref[:, PACK:FULL, :] = jnp.zeros((col_span, FULL - PACK, TILE), jnp.bfloat16)

    def copies(sources, target, sems):
        size = target.shape[0] // len(sources)
        return [
            pltpu.make_async_copy(source, target.at[pl.ds(at * size, size), pl.ds(0, PACK)], sems.at[at])
            for at, source in enumerate(sources)
        ]

    row_copies = copies(rows_from, rows_ref, row_sems)
    col_copies = copies(cols_from, cols_ref, col_sems)
    for copy in row_copies + col_copies:
        copy.start()

    fsum_ref[...] = jnp.zeros_like(fsum_ref)
    msum_ref[...] = jnp.zeros_like(msum_ref)

    part = row_span // ROW_PARTS
    for at, copy in enumerate(row_copies):
        copy.wait()

        @pl.loop(at * part, (at + 1) * part)
        def _(block):
            turned_ref[block, :, 0:DESC] = rows_ref[block, 0:DESC, :].T
            offsets = rows_ref[block, DESC:DEPTH, :]
            padded = jnp.concatenate([offsets, jnp.zeros((FULL - DEPTH, TILE), jnp.bfloat16)], axis=0)
            turned_ref[block, :, DESC:FULL] = padded.T

    for copy in col_copies:
        copy.wait()

    def tile(slot):
        row_at = slots_ref[0, slot]
        col_at = slots_ref[1, slot]
        score = jnp.dot(turned_ref[row_at], cols_ref[col_at], preferred_element_type=jnp.float32)
        block = jnp.exp2(score * POWER).astype(jnp.bfloat16)
        forward = lax.dot_general(
            cols_ref[col_at, DEPTH:PACK, :], block, (((1,), (1,)), ((), ())), preferred_element_type=jnp.float32
        )
        mirror = jnp.dot(rows_ref[row_at, DEPTH:PACK, :], block, preferred_element_type=jnp.float32)
        return slots_ref[2, slot], slots_ref[3, slot], forward, mirror

    @pl.loop(0, lax.div(count_ref[0, 0] + (UNROLL - 1), UNROLL))
    def _(group):
        done = [tile(group * UNROLL + step) for step in range(UNROLL)]
        for forward_at, mirror_at, forward, mirror in done:
            fsum_ref[forward_at] += forward
            msum_ref[mirror_at] += mirror

    half = row_span // 2
    forward_ref[...] = fsum_ref[0:half]
    other_ref[...] = fsum_ref[half:row_span].astype(jnp.bfloat16)
    mirror_ref[...] = msum_ref[0:col_span].astype(jnp.bfloat16)


def tile_products(slots, tile_count, row_parts, col_parts):
    row_span = sum(part.shape[0] for part in row_parts)
    col_span = sum(part.shape[0] for part in col_parts)
    smem = pl.BlockSpec(memory_space=pltpu.SMEM)
    vmem = pl.BlockSpec(memory_space=pltpu.VMEM)
    anywhere = pl.BlockSpec(memory_space=pl.ANY)
    return pl.pallas_call(
        tiles_kernel,
        out_shape=(
            jax.ShapeDtypeStruct((row_span // 2, VECS, TILE), jnp.float32),
            jax.ShapeDtypeStruct((row_span // 2, VECS, TILE), jnp.bfloat16),
            jax.ShapeDtypeStruct((col_span, VECS, TILE), jnp.bfloat16),
        ),
        in_specs=[smem, smem] + [anywhere] * (ROW_PARTS + COL_PARTS),
        out_specs=(vmem, vmem, vmem),
        scratch_shapes=[
            pltpu.VMEM((row_span, PACK, TILE), jnp.bfloat16),
            pltpu.VMEM((col_span, FULL, TILE), jnp.bfloat16),
            pltpu.VMEM((row_span, TILE, FULL), jnp.bfloat16),
            pltpu.VMEM((row_span + 1, VECS, TILE), jnp.float32),
            pltpu.VMEM((col_span + 1, VECS, TILE), jnp.float32),
            pltpu.SemaphoreType.DMA((ROW_PARTS,)),
            pltpu.SemaphoreType.DMA((COL_PARTS,)),
        ],
        compiler_params=pltpu.CompilerParams(vmem_limit_bytes=48 * 1024 * 1024),
        name="tile_products",
    )(slots, tile_count, *row_parts, *col_parts)


def shifted(value, axis, sizes, part, distance):
    pairs = []
    for source in range(math.prod(sizes)):
        place = list(split_index(source, sizes))
        place[part] = (place[part] + distance) % sizes[part]
        target = 0
        for at, size in zip(place, sizes):
            target = target * size + at
        pairs.append((source, target))
    return lax.ppermute(value, axis, pairs)


def split_index(index, sizes):
    place = []
    for size in reversed(sizes):
        place.append(index & (size - 1))
        index = index >> (size.bit_length() - 1)
    return tuple(reversed(place))


def gather_rows(own):
    along_y = jnp.stack([own] + [shifted(own, "col", COL_SIZES, 0, step) for step in range(1, 4)])
    parts = [along_y] + [shifted(along_y, "col", COL_SIZES, 1, step) for step in range(1, 4)]
    return parts + [shifted(part, "col", COL_SIZES, 2, 1) for part in parts]


def grouped_all_to_all(value, axis, sizes, part_of):
    groups = {}
    for index in range(math.prod(sizes)):
        groups.setdefault(part_of(split_index(index, sizes)), []).append(index)
    return lax.all_to_all(value, axis, 0, 0, axis_index_groups=list(groups.values()), tiled=True)


def gather_pair(own):
    pair = jnp.stack([own, shifted(own, "row", ROW_SIZES, 0, 1)])
    return jnp.broadcast_to(pair[None], (ROW_SIZES[1],) + pair.shape).reshape((-1,) + own.shape)


def gather_cols(pairs):
    return [grouped_all_to_all(pairs, "row", ROW_SIZES, lambda place: place[0])]


def slot_places(tile_pairs, tile_count):
    row_span = math.prod(COL_SIZES)
    col_span = math.prod(ROW_SIZES)
    i, j = tile_pairs[0], tile_pairs[1]
    local_row, local_col = lax.rem(i, row_span), lax.div(j, row_span)

    row_here, row_there = split_index(lax.axis_index("row"), ROW_SIZES), split_index(local_col, ROW_SIZES)
    col_here, col_there = split_index(lax.axis_index("col"), COL_SIZES), split_index(local_row, COL_SIZES)
    y_hi, x, core = [(mine - other) & (size - 1) for mine, other, size in zip(col_here, col_there, COL_SIZES)]
    live = jnp.arange(tile_pairs.shape[1], dtype=jnp.int32) < tile_count
    return jnp.stack(
        [
            (core * 4 + x) * 4 + y_hi,
            row_there[1] * 2 + (row_there[0] ^ row_here[0]),
            jnp.where(live, core * (row_span // 2) + (local_row >> 1), row_span),
            jnp.where(live & (i != j), local_col, col_span),
        ]
    )


def body(features, scales, vectors, pattern, counts):
    row_own, col_own = pack_blocks(features, scales, vectors)
    pairs, row_own = lax.optimization_barrier((gather_pair(col_own), row_own))
    col_parts = gather_cols(pairs)
    row_parts = gather_rows(row_own)
    slots = slot_places(pattern[0, 0], counts[0, 0])
    forward, for_other_core, mirror = tile_products(slots, counts, row_parts, col_parts)
    for_other_core = shifted(for_other_core, "col", COL_SIZES, 2, 1)
    mirror = lax.all_to_all(mirror, "row", 0, 0, tiled=True)
    forward = (forward + for_other_core.astype(jnp.float32)).astype(jnp.bfloat16)
    forward = grouped_all_to_all(forward, "col", COL_SIZES, lambda place: place[2])
    return jnp.sum(forward.astype(jnp.float32), axis=0) + jnp.sum(mirror.astype(jnp.float32), axis=0)


def solution(mesh):
    placed = (
        P(("row", "col"), None),
        P(("row", "col")),
        P(None, ("row", "col")),
        P("row", "col", None, None),
        P("row", "col"),
    )
    return jax.shard_map(
        body, mesh=mesh, in_specs=placed, out_specs=P(None, ("row", "col")), check_vma=False
    )
```

```python
import math

import jax
import jax.numpy as jnp
from jax import lax
from jax.experimental import pallas as pl
from jax.experimental.pallas import tpu as pltpu
from jax.sharding import PartitionSpec as P

TILE = 256
DESC = 128
VECS = 32
AUG = 16
DEPTH = DESC + AUG
PACK = DEPTH + VECS
FULL = 256
LANES = 128
UNROLL = 8

COL_SIZES = (4, 4, 2)
ROW_SIZES = (2, 8)
ROW_PARTS = 8
COL_PARTS = 2

POWER = math.log2(math.e) * 2.0 / DESC


def pack_kernel(feat_ref, scale_ref, vec_ref, row_ref, col_ref):
    turned = feat_ref[...].astype(jnp.float32).T
    norm = jnp.sum(turned * turned, axis=0, keepdims=True)
    offset = (DESC // 2) * jnp.log(scale_ref[...].astype(jnp.float32)) - 0.5 * norm
    high = offset.astype(jnp.bfloat16).astype(jnp.float32)
    rest = offset - high
    middle = rest.astype(jnp.bfloat16).astype(jnp.float32)
    low = (rest - middle).astype(jnp.bfloat16).astype(jnp.float32)
    place = lax.broadcasted_iota(jnp.int32, (AUG, TILE), 0)

    def offset_rows(first_own, first_one):
        own = place - first_own
        rows = jnp.where(own == 0, high, jnp.where(own == 1, middle, jnp.where(own == 2, low, 0.0)))
        one = place - first_one
        return jnp.where((one >= 0) & (one < 3), 1.0, rows).astype(jnp.bfloat16)

    descriptors = turned.astype(jnp.bfloat16)
    narrow = vec_ref[...].astype(jnp.bfloat16)
    row_offsets, col_offsets = offset_rows(0, 3), offset_rows(3, 0)
    row_ref[0:DESC, :] = descriptors
    row_ref[DESC:DEPTH, :] = row_offsets
    row_ref[DEPTH:PACK, :] = narrow
    for copy in range(col_ref.shape[0]):
        col_ref[copy, 0:DESC, :] = descriptors
        col_ref[copy, DESC:DEPTH, :] = col_offsets
        col_ref[copy, DEPTH:PACK, :] = narrow


def pack_blocks(features, scales, vectors):
    shapes = (
        jax.ShapeDtypeStruct((PACK, TILE), jnp.bfloat16),
        jax.ShapeDtypeStruct((ROW_SIZES[1], PACK, TILE), jnp.bfloat16),
    )
    return pl.pallas_call(pack_kernel, out_shape=shapes, name="pack_blocks")(
        features, scales.reshape(1, TILE), vectors
    )


def tiles_kernel(slots_ref, count_ref, *refs):
    rows_from, cols_from = refs[:ROW_PARTS], refs[ROW_PARTS : ROW_PARTS + COL_PARTS]
    forward_ref, forward_other_ref, mirror_ref, mirror_other_ref = refs[ROW_PARTS + COL_PARTS :][:4]
    rows_ref, cols_ref, turned_ref, vecs_ref, fsum_ref, msum_ref, row_sems, col_sems = refs[ROW_PARTS + COL_PARTS + 4 :]
    row_span = rows_ref.shape[0]
    col_span = cols_ref.shape[0]

    cols_ref[:, PACK:FULL, :] = jnp.zeros((col_span, FULL - PACK, TILE), jnp.bfloat16)

    def copies(sources, target, sems):
        size = target.shape[0] // len(sources)
        return [
            pltpu.make_async_copy(source, target.at[pl.ds(at * size, size), pl.ds(0, PACK)], sems.at[at])
            for at, source in enumerate(sources)
        ]

    row_copies = copies(rows_from, rows_ref, row_sems)
    col_copies = copies(cols_from, cols_ref, col_sems)
    for copy in row_copies + col_copies:
        copy.start()

    fsum_ref[...] = jnp.zeros_like(fsum_ref)
    msum_ref[...] = jnp.zeros_like(msum_ref)

    part = row_span // ROW_PARTS
    for at, copy in enumerate(row_copies):
        copy.wait()

        @pl.loop(at * part, (at + 1) * part)
        def _(block):
            turned_ref[block, :, 0:DESC] = rows_ref[block, 0:DESC, :].T
            offsets = rows_ref[block, DESC:DEPTH, :]
            padded = jnp.concatenate([offsets, jnp.zeros((FULL - DEPTH, TILE), jnp.bfloat16)], axis=0)
            turned_ref[block, :, DESC:FULL] = padded.T

    for copy in col_copies:
        copy.wait()

    @pl.loop(0, col_span)
    def _(block):
        narrow = cols_ref[block, DEPTH:PACK, :]
        vecs_ref[block] = jnp.concatenate([narrow, jnp.zeros((LANES - VECS, TILE), jnp.bfloat16)], axis=0).T

    def tile(slot):
        row_at = slots_ref[0, slot]
        col_at = slots_ref[1, slot]
        score = jnp.dot(turned_ref[row_at], cols_ref[col_at], preferred_element_type=jnp.float32)
        block = jnp.exp2(score * POWER).astype(jnp.bfloat16)
        forward = jnp.dot(block, vecs_ref[col_at], preferred_element_type=jnp.float32)
        mirror = jnp.dot(rows_ref[row_at, DEPTH:PACK, :], block, preferred_element_type=jnp.float32)
        return slots_ref[2, slot], slots_ref[3, slot], forward, mirror

    @pl.loop(0, lax.div(count_ref[0, 0] + (UNROLL - 1), UNROLL))
    def _(group):
        done = [tile(group * UNROLL + step) for step in range(UNROLL)]
        for forward_at, mirror_at, forward, mirror in done:
            fsum_ref[forward_at] += forward
            msum_ref[mirror_at] += mirror

    half = row_span // 2

    @pl.loop(0, half)
    def _(block):
        forward_ref[block] = fsum_ref[block].T[0:VECS]
        forward_other_ref[block] = fsum_ref[half + block].T[0:VECS].astype(jnp.bfloat16)

    mirror_ref[...] = msum_ref[0 : col_span // 2]
    mirror_other_ref[...] = msum_ref[col_span // 2 : col_span].astype(jnp.bfloat16)


def tile_products(slots, tile_count, row_parts, col_parts):
    row_span = sum(part.shape[0] for part in row_parts)
    col_span = sum(part.shape[0] for part in col_parts)
    smem = pl.BlockSpec(memory_space=pltpu.SMEM)
    vmem = pl.BlockSpec(memory_space=pltpu.VMEM)
    anywhere = pl.BlockSpec(memory_space=pl.ANY)
    return pl.pallas_call(
        tiles_kernel,
        out_shape=(
            jax.ShapeDtypeStruct((row_span // 2, VECS, TILE), jnp.float32),
            jax.ShapeDtypeStruct((row_span // 2, VECS, TILE), jnp.bfloat16),
            jax.ShapeDtypeStruct((col_span // 2, VECS, TILE), jnp.float32),
            jax.ShapeDtypeStruct((col_span // 2, VECS, TILE), jnp.bfloat16),
        ),
        in_specs=[smem, smem] + [anywhere] * (ROW_PARTS + COL_PARTS),
        out_specs=(vmem, vmem, vmem, vmem),
        scratch_shapes=[
            pltpu.VMEM((row_span, PACK, TILE), jnp.bfloat16),
            pltpu.VMEM((col_span, FULL, TILE), jnp.bfloat16),
            pltpu.VMEM((row_span, TILE, FULL), jnp.bfloat16),
            pltpu.VMEM((col_span, TILE, LANES), jnp.bfloat16),
            pltpu.VMEM((row_span + 1, TILE, LANES), jnp.float32),
            pltpu.VMEM((col_span + 1, VECS, TILE), jnp.float32),
            pltpu.SemaphoreType.DMA((ROW_PARTS,)),
            pltpu.SemaphoreType.DMA((COL_PARTS,)),
        ],
        compiler_params=pltpu.CompilerParams(vmem_limit_bytes=48 * 1024 * 1024),
        name="tile_products",
    )(slots, tile_count, *row_parts, *col_parts)


def moved(value, axis, sizes, part, place_to):
    pairs = []
    for source in range(math.prod(sizes)):
        place = list(split_index(source, sizes))
        place[part] = place_to(place[part])
        target = 0
        for at, size in zip(place, sizes):
            target = target * size + at
        pairs.append((source, target))
    return lax.ppermute(value, axis, pairs)


def shifted(value, axis, sizes, part, distance):
    return moved(value, axis, sizes, part, lambda place: (place + distance) % sizes[part])


def swapped(value, axis, sizes, part, bit):
    return moved(value, axis, sizes, part, lambda place: place ^ bit)


def split_index(index, sizes):
    place = []
    for size in reversed(sizes):
        place.append(index & (size - 1))
        index = index >> (size.bit_length() - 1)
    return tuple(reversed(place))


def gather_rows(own):
    along_y = jnp.stack([own] + [shifted(own, "col", COL_SIZES, 0, step) for step in range(1, 4)])
    parts = [along_y] + [shifted(along_y, "col", COL_SIZES, 1, step) for step in range(1, 4)]
    return parts + [shifted(part, "col", COL_SIZES, 2, 1) for part in parts]


def grouped_all_to_all(value, axis, sizes, part_of):
    groups = {}
    for index in range(math.prod(sizes)):
        groups.setdefault(part_of(split_index(index, sizes)), []).append(index)
    return lax.all_to_all(value, axis, 0, 0, axis_index_groups=list(groups.values()), tiled=True)


def gather_cols(copies):
    along_z = grouped_all_to_all(copies, "row", ROW_SIZES, lambda place: place[0])
    return [along_z, swapped(along_z, "row", ROW_SIZES, 0, 1)]


def add_mirrors(mirror, for_neighbour, after):
    mirror = mirror + swapped(for_neighbour, "row", ROW_SIZES, 0, 1).astype(jnp.float32)
    bit = ROW_SIZES[1] // 2
    while bit:
        sent = mirror[bit:].astype(jnp.bfloat16) if bit > 2 else mirror[bit:]
        sent, _ = lax.optimization_barrier((sent, after))
        mirror = mirror[:bit] + swapped(sent, "row", ROW_SIZES, 1, bit).astype(jnp.float32)
        bit //= 2
    return mirror[0]


def slot_places(tile_pairs, tile_count):
    row_span = math.prod(COL_SIZES)
    col_span = math.prod(ROW_SIZES)
    i, j = tile_pairs[0], tile_pairs[1]
    local_row, local_col = lax.rem(i, row_span), lax.div(j, row_span)

    row_here, row_there = split_index(lax.axis_index("row"), ROW_SIZES), split_index(local_col, ROW_SIZES)
    col_here, col_there = split_index(lax.axis_index("col"), COL_SIZES), split_index(local_row, COL_SIZES)
    y_hi, x, core = [(mine - other) & (size - 1) for mine, other, size in zip(col_here, col_there, COL_SIZES)]
    live = jnp.arange(tile_pairs.shape[1], dtype=jnp.int32) < tile_count
    return jnp.stack(
        [
            (core * 4 + x) * 4 + y_hi,
            (row_there[0] ^ row_here[0]) * (col_span // 2) + row_there[1],
            jnp.where(live, core * (row_span // 2) + (local_row >> 1), row_span),
            jnp.where(live & (i != j), local_col ^ lax.axis_index("row"), col_span),
        ]
    )


def body(features, scales, vectors, pattern, counts):
    row_own, col_copies = pack_blocks(features, scales, vectors)
    col_parts = gather_cols(col_copies)
    row_parts = gather_rows(row_own)
    slots = slot_places(pattern[0, 0], counts[0, 0])
    forward, for_other_core, mirror, for_neighbour = tile_products(slots, counts, row_parts, col_parts)
    for_other_core = swapped(for_other_core, "col", COL_SIZES, 2, 1)
    forward = (forward + for_other_core.astype(jnp.float32)).astype(jnp.bfloat16)
    mirror = add_mirrors(mirror, for_neighbour, forward)
    forward = grouped_all_to_all(forward, "col", COL_SIZES, lambda place: place[2])
    return jnp.sum(forward.astype(jnp.float32), axis=0) + mirror


def solution(mesh):
    placed = (
        P(("row", "col"), None),
        P(("row", "col")),
        P(None, ("row", "col")),
        P("row", "col", None, None),
        P("row", "col"),
    )
    return jax.shard_map(
        body, mesh=mesh, in_specs=placed, out_specs=P(None, ("row", "col")), check_vma=False
    )
```

```python
import math

import jax
import jax.numpy as jnp
from jax import lax
from jax.experimental import pallas as pl
from jax.experimental.pallas import tpu as pltpu
from jax.sharding import PartitionSpec as P

TILE = 256
DESC = 128
VECS = 32
AUG = 16
DEPTH = DESC + AUG
PACK = DEPTH + VECS
FULL = 256
LANES = 128
AUG_GROUP = LANES // AUG
VEC_GROUP = LANES // VECS
UNROLL = 8

COL_SIZES = (4, 4, 2)
ROW_SIZES = (2, 8)
ROW_PARTS = 8
COL_PARTS = 2

POWER = math.log2(math.e) * 2.0 / DESC


def pack_kernel(feat_ref, scale_ref, vec_ref, row_ref, col_ref):
    turned = feat_ref[...].astype(jnp.float32).T
    norm = jnp.sum(turned * turned, axis=0, keepdims=True)
    offset = (DESC // 2) * jnp.log(scale_ref[...].astype(jnp.float32).reshape(1, TILE)) - 0.5 * norm
    high = offset.astype(jnp.bfloat16).astype(jnp.float32)
    rest = offset - high
    middle = rest.astype(jnp.bfloat16).astype(jnp.float32)
    low = (rest - middle).astype(jnp.bfloat16).astype(jnp.float32)
    place = lax.broadcasted_iota(jnp.int32, (AUG, TILE), 0)

    def offset_rows(first_own, first_one):
        own = place - first_own
        rows = jnp.where(own == 0, high, jnp.where(own == 1, middle, jnp.where(own == 2, low, 0.0)))
        one = place - first_one
        return jnp.where((one >= 0) & (one < 3), 1.0, rows).astype(jnp.bfloat16)

    descriptors = turned.astype(jnp.bfloat16)
    narrow = vec_ref[...].astype(jnp.bfloat16)
    row_offsets, col_offsets = offset_rows(0, 3), offset_rows(3, 0)
    row_ref[0:DESC, 0:DESC] = feat_ref[0:DESC, :]
    row_ref[0:DESC, DESC:TILE] = feat_ref[DESC:TILE, :]
    row_ref[DESC:DEPTH, :] = row_offsets
    row_ref[DEPTH:PACK, :] = narrow
    for copy in range(col_ref.shape[0]):
        col_ref[copy, 0:DESC, :] = descriptors
        col_ref[copy, DESC:DEPTH, :] = col_offsets
        col_ref[copy, DEPTH:PACK, :] = narrow


def pack_blocks(features, scales, vectors):
    shapes = (
        jax.ShapeDtypeStruct((PACK, TILE), jnp.bfloat16),
        jax.ShapeDtypeStruct((ROW_SIZES[1], PACK, TILE), jnp.bfloat16),
    )
    return pl.pallas_call(pack_kernel, out_shape=shapes, name="pack_blocks")(
        features, scales, vectors
    )


def tiles_kernel(slots_ref, count_ref, *refs):
    rows_from, cols_from = refs[:ROW_PARTS], refs[ROW_PARTS : ROW_PARTS + COL_PARTS]
    forward_ref, forward_other_ref, mirror_ref, mirror_other_ref = refs[ROW_PARTS + COL_PARTS :][:4]
    rows_ref, cols_ref, cvecs_ref, left_ref, vecs_ref, fsum_ref, msum_ref, row_sems, col_sems, vec_sems = refs[ROW_PARTS + COL_PARTS + 4 :]
    row_span = rows_ref.shape[0]
    col_span = cols_ref.shape[0]

    def copies(sources, target, sems, first, last):
        size = target.shape[0] // len(sources)
        return [
            pltpu.make_async_copy(
                source.at[:, pl.ds(first, last - first)], target.at[pl.ds(at * size, size), pl.ds(0, last - first)], sems.at[at]
            )
            for at, source in enumerate(sources)
        ]

    row_copies = copies(rows_from, rows_ref, row_sems, 0, PACK)
    col_copies = copies(cols_from, cols_ref, col_sems, 0, DEPTH)
    vec_copies = copies(cols_from, cvecs_ref, vec_sems, DEPTH, PACK)
    for copy in row_copies + col_copies + vec_copies:
        copy.start()

    fsum_ref[...] = jnp.zeros_like(fsum_ref)
    msum_ref[...] = jnp.zeros_like(msum_ref)
    lane = lax.broadcasted_iota(jnp.int32, (TILE, LANES), 1)

    def lanes_of(group, width):
        return jnp.where(lax.div(lane, width) == group, 1.0, 0.0).astype(jnp.bfloat16)

    for copy in row_copies:
        copy.wait()

    @pl.loop(0, row_span)
    def _(block):
        left_ref[block, 0:DESC, 0:DESC] = rows_ref[block, 0:DESC, 0:DESC]
        left_ref[block, DESC:TILE, 0:DESC] = rows_ref[block, 0:DESC, DESC:TILE]

    @pl.loop(0, row_span // AUG_GROUP)
    def _(group):
        offsets = rows_ref[pl.ds(group * AUG_GROUP, AUG_GROUP), DESC:DEPTH, :].reshape(LANES, TILE).T
        for at in range(AUG_GROUP):
            left_ref[group * AUG_GROUP + at, :, DESC:FULL] = offsets * lanes_of(at, AUG)

    for copy in col_copies + vec_copies:
        copy.wait()

    @pl.loop(0, col_span)
    def _(block):
        offsets = cols_ref[block, DESC:DEPTH, :]
        for at in range(1, AUG_GROUP):
            cols_ref[block, DESC + at * AUG : DESC + (at + 1) * AUG, :] = offsets

    @pl.loop(0, col_span // VEC_GROUP)
    def _(group):
        narrow = cvecs_ref[pl.ds(group * VEC_GROUP, VEC_GROUP)].reshape(LANES, TILE).T
        for at in range(VEC_GROUP):
            vecs_ref[group * VEC_GROUP + at] = narrow * lanes_of(at, VECS)

    def tile(slot):
        row_at = slots_ref[0, slot]
        col_at = slots_ref[1, slot]
        score = jnp.dot(left_ref[row_at], cols_ref[col_at], preferred_element_type=jnp.float32)
        block = jnp.exp2(score * POWER).astype(jnp.bfloat16)
        forward = jnp.dot(block, vecs_ref[col_at], preferred_element_type=jnp.float32)
        mirror = jnp.dot(rows_ref[row_at, DEPTH:PACK, :], block, preferred_element_type=jnp.float32)
        return slots_ref[2, slot], slots_ref[3, slot], forward, mirror

    @pl.loop(0, lax.div(count_ref[0, 0] + (UNROLL - 1), UNROLL))
    def _(group):
        done = [tile(group * UNROLL + step) for step in range(UNROLL)]
        for forward_at, mirror_at, forward, mirror in done:
            fsum_ref[forward_at] += forward
            msum_ref[mirror_at] += mirror

    half = row_span // 2

    def total(block):
        turned = fsum_ref[block].T
        return sum(turned[at * VECS : (at + 1) * VECS] for at in range(VEC_GROUP))

    @pl.loop(0, half)
    def _(block):
        forward_ref[block] = total(block)
        forward_other_ref[block] = total(half + block).astype(jnp.bfloat16)

    mirror_ref[...] = msum_ref[0 : col_span // 2]
    mirror_other_ref[...] = msum_ref[col_span // 2 : col_span].astype(jnp.bfloat16)


def tile_products(slots, tile_count, row_parts, col_parts):
    row_span = sum(part.shape[0] for part in row_parts)
    col_span = sum(part.shape[0] for part in col_parts)
    smem = pl.BlockSpec(memory_space=pltpu.SMEM)
    vmem = pl.BlockSpec(memory_space=pltpu.VMEM)
    anywhere = pl.BlockSpec(memory_space=pl.ANY)
    return pl.pallas_call(
        tiles_kernel,
        out_shape=(
            jax.ShapeDtypeStruct((row_span // 2, VECS, TILE), jnp.float32),
            jax.ShapeDtypeStruct((row_span // 2, VECS, TILE), jnp.bfloat16),
            jax.ShapeDtypeStruct((col_span // 2, VECS, TILE), jnp.float32),
            jax.ShapeDtypeStruct((col_span // 2, VECS, TILE), jnp.bfloat16),
        ),
        in_specs=[smem, smem] + [anywhere] * (ROW_PARTS + COL_PARTS),
        out_specs=(vmem, vmem, vmem, vmem),
        scratch_shapes=[
            pltpu.VMEM((row_span, PACK, TILE), jnp.bfloat16),
            pltpu.VMEM((col_span, FULL, TILE), jnp.bfloat16),
            pltpu.VMEM((col_span, VECS, TILE), jnp.bfloat16),
            pltpu.VMEM((row_span, TILE, FULL), jnp.bfloat16),
            pltpu.VMEM((col_span, TILE, LANES), jnp.bfloat16),
            pltpu.VMEM((row_span + 1, TILE, LANES), jnp.float32),
            pltpu.VMEM((col_span + 1, VECS, TILE), jnp.float32),
            pltpu.SemaphoreType.DMA((ROW_PARTS,)),
            pltpu.SemaphoreType.DMA((COL_PARTS,)),
            pltpu.SemaphoreType.DMA((COL_PARTS,)),
        ],
        compiler_params=pltpu.CompilerParams(vmem_limit_bytes=48 * 1024 * 1024),
        name="tile_products",
    )(slots, tile_count, *row_parts, *col_parts)


def moved(value, axis, sizes, part, place_to):
    pairs = []
    for source in range(math.prod(sizes)):
        place = list(split_index(source, sizes))
        place[part] = place_to(place[part])
        target = 0
        for at, size in zip(place, sizes):
            target = target * size + at
        pairs.append((source, target))
    return lax.ppermute(value, axis, pairs)


def shifted(value, axis, sizes, part, distance):
    return moved(value, axis, sizes, part, lambda place: (place + distance) % sizes[part])


def swapped(value, axis, sizes, part, bit):
    return moved(value, axis, sizes, part, lambda place: place ^ bit)


def split_index(index, sizes):
    place = []
    for size in reversed(sizes):
        place.append(index & (size - 1))
        index = index >> (size.bit_length() - 1)
    return tuple(reversed(place))


def gather_rows(own):
    along_y = jnp.stack([own] + [shifted(own, "col", COL_SIZES, 0, step) for step in range(1, 4)])
    parts = [along_y] + [shifted(along_y, "col", COL_SIZES, 1, step) for step in range(1, 4)]
    return parts + [shifted(part, "col", COL_SIZES, 2, 1) for part in parts]


def grouped_all_to_all(value, axis, sizes, part_of):
    groups = {}
    for index in range(math.prod(sizes)):
        groups.setdefault(part_of(split_index(index, sizes)), []).append(index)
    return lax.all_to_all(value, axis, 0, 0, axis_index_groups=list(groups.values()), tiled=True)


def gather_cols(copies):
    along_z = grouped_all_to_all(copies, "row", ROW_SIZES, lambda place: place[0])
    return [along_z, swapped(along_z, "row", ROW_SIZES, 0, 1)]


def add_mirrors(mirror, for_neighbour, after):
    received, _ = lax.optimization_barrier((swapped(for_neighbour, "row", ROW_SIZES, 0, 1), after))
    mirror = mirror + received.astype(jnp.float32)
    bit = ROW_SIZES[1] // 2
    while bit:
        sent = mirror[bit:].astype(jnp.bfloat16) if bit > 2 else mirror[bit:]
        sent, _ = lax.optimization_barrier((sent, after))
        mirror = mirror[:bit] + swapped(sent, "row", ROW_SIZES, 1, bit).astype(jnp.float32)
        bit //= 2
    return mirror[0]


def slot_places(tile_pairs, tile_count):
    row_span = math.prod(COL_SIZES)
    col_span = math.prod(ROW_SIZES)
    i, j = tile_pairs[0], tile_pairs[1]
    local_row, local_col = lax.rem(i, row_span), lax.div(j, row_span)

    row_here, row_there = split_index(lax.axis_index("row"), ROW_SIZES), split_index(local_col, ROW_SIZES)
    col_here, col_there = split_index(lax.axis_index("col"), COL_SIZES), split_index(local_row, COL_SIZES)
    y_hi, x, core = [(mine - other) & (size - 1) for mine, other, size in zip(col_here, col_there, COL_SIZES)]
    live = jnp.arange(tile_pairs.shape[1], dtype=jnp.int32) < tile_count
    return jnp.stack(
        [
            (core * 4 + x) * 4 + y_hi,
            (row_there[0] ^ row_here[0]) * (col_span // 2) + row_there[1],
            jnp.where(live, core * (row_span // 2) + (local_row >> 1), row_span),
            jnp.where(live & (i != j), local_col ^ lax.axis_index("row"), col_span),
        ]
    )


def body(features, scales, vectors, pattern, counts):
    row_own, col_copies = pack_blocks(features, scales, vectors)
    col_parts = gather_cols(col_copies)
    row_parts = gather_rows(row_own)
    slots = slot_places(pattern[0, 0], counts[0, 0])
    forward, for_other_core, mirror, for_neighbour = tile_products(slots, counts, row_parts, col_parts)
    for_other_core = swapped(for_other_core, "col", COL_SIZES, 2, 1)
    forward = (forward + for_other_core.astype(jnp.float32)).astype(jnp.bfloat16)
    mirror = add_mirrors(mirror, for_neighbour, forward)
    forward = grouped_all_to_all(forward, "col", COL_SIZES, lambda place: place[2])
    return jnp.sum(forward.astype(jnp.float32), axis=0) + mirror


def solution(mesh):
    placed = (
        P(("row", "col"), None),
        P(("row", "col")),
        P(None, ("row", "col")),
        P("row", "col", None, None),
        P("row", "col"),
    )
    return jax.shard_map(
        body, mesh=mesh, in_specs=placed, out_specs=P(None, ("row", "col")), check_vma=False
    )
```

```python
import math

import jax
import jax.numpy as jnp
from jax import lax
from jax.experimental import pallas as pl
from jax.experimental.pallas import tpu as pltpu
from jax.sharding import PartitionSpec as P

TILE = 256
DESC = 128
VECS = 32
AUG = 16
DEPTH = DESC + AUG
PACK = DEPTH + VECS
FULL = 256
LANES = 128
AUG_GROUP = LANES // AUG
VEC_GROUP = LANES // VECS
UNROLL = 16

COL_SIZES = (4, 4, 2)
ROW_SIZES = (2, 8)
ROW_PARTS = 8
COL_PARTS = 2

POWER = math.log2(math.e) * 2.0 / DESC


def pack_kernel(feat_ref, scale_ref, vec_ref, row_ref, col_ref):
    turned = feat_ref[...].astype(jnp.float32).T
    norm = jnp.sum(turned * turned, axis=0, keepdims=True)
    offset = (DESC // 2) * jnp.log(scale_ref[...].astype(jnp.float32).reshape(1, TILE)) - 0.5 * norm
    high = offset.astype(jnp.bfloat16).astype(jnp.float32)
    rest = offset - high
    middle = rest.astype(jnp.bfloat16).astype(jnp.float32)
    low = (rest - middle).astype(jnp.bfloat16).astype(jnp.float32)
    place = lax.broadcasted_iota(jnp.int32, (AUG, TILE), 0)

    def offset_rows(first_own, first_one):
        own = place - first_own
        rows = jnp.where(own == 0, high, jnp.where(own == 1, middle, jnp.where(own == 2, low, 0.0)))
        one = place - first_one
        return jnp.where((one >= 0) & (one < 3), 1.0, rows).astype(jnp.bfloat16)

    descriptors = turned.astype(jnp.bfloat16)
    narrow = vec_ref[...].astype(jnp.bfloat16)
    row_offsets, col_offsets = offset_rows(0, 3), offset_rows(3, 0)
    row_ref[0:DESC, 0:DESC] = feat_ref[0:DESC, :]
    row_ref[0:DESC, DESC:TILE] = feat_ref[DESC:TILE, :]
    row_ref[DESC:DEPTH, :] = row_offsets
    row_ref[DEPTH:PACK, :] = narrow
    for copy in range(col_ref.shape[0]):
        col_ref[copy, 0:DESC, :] = descriptors
        col_ref[copy, DESC:DEPTH, :] = col_offsets
        col_ref[copy, DEPTH:PACK, :] = narrow


def pack_blocks(features, scales, vectors):
    shapes = (
        jax.ShapeDtypeStruct((PACK, TILE), jnp.bfloat16),
        jax.ShapeDtypeStruct((ROW_SIZES[1], PACK, TILE), jnp.bfloat16),
    )
    return pl.pallas_call(pack_kernel, out_shape=shapes, name="pack_blocks")(
        features, scales, vectors
    )


def tiles_kernel(slots_ref, count_ref, *refs):
    rows_from, cols_from = refs[:ROW_PARTS], refs[ROW_PARTS : ROW_PARTS + COL_PARTS]
    forward_ref, mirror_ref, mirror_other_ref = refs[ROW_PARTS + COL_PARTS :][:3]
    left_ref, row_vecs_ref, right_ref, col_vecs_ref, turned_ref, fsum_ref, msum_ref = refs[ROW_PARTS + COL_PARTS + 3 :]
    row_span = left_ref.shape[0]
    col_span = right_ref.shape[0]

    fsum_ref[...] = jnp.zeros_like(fsum_ref)
    msum_ref[...] = jnp.zeros_like(msum_ref)
    lane = lax.broadcasted_iota(jnp.int32, (TILE, LANES), 1)

    def lanes_of(group, width):
        return jnp.where(lax.div(lane, width) == group, 1.0, 0.0).astype(jnp.bfloat16)

    offset_rows = []
    for at, part in enumerate(rows_from):
        size = part.shape[0]
        for own in range(size):
            block = at * size + own
            left_ref[block, 0:DESC, 0:DESC] = part[own, 0:DESC, 0:DESC]
            left_ref[block, DESC:TILE, 0:DESC] = part[own, 0:DESC, DESC:TILE]
            row_vecs_ref[block] = part[own, DEPTH:PACK, :]
            offset_rows.append(part[own, DESC:DEPTH, :])
            if len(offset_rows) == AUG_GROUP:
                turned = jnp.concatenate(offset_rows, axis=0).T
                for place in range(AUG_GROUP):
                    left_ref[block - AUG_GROUP + 1 + place, :, DESC:FULL] = turned * lanes_of(place, AUG)
                offset_rows = []

    for at, part in enumerate(cols_from):
        size = part.shape[0]

        @pl.loop(0, size)
        def _(own):
            right_ref[at * size + own, 0:DESC, :] = part[own, 0:DESC, :]
            offsets = part[own, DESC:DEPTH, :]
            for place in range(AUG_GROUP):
                right_ref[at * size + own, DESC + place * AUG : DESC + (place + 1) * AUG, :] = offsets
            col_vecs_ref[at * size + own] = part[own, DEPTH:PACK, :]

    @pl.loop(0, col_span // VEC_GROUP)
    def _(group):
        narrow = col_vecs_ref[pl.ds(group * VEC_GROUP, VEC_GROUP)].reshape(LANES, TILE).T
        for at in range(VEC_GROUP):
            turned_ref[group * VEC_GROUP + at] = narrow * lanes_of(at, VECS)

    def tile(slot):
        row_at = slots_ref[0, slot]
        col_at = slots_ref[1, slot]
        score = jnp.dot(left_ref[row_at], right_ref[col_at], preferred_element_type=jnp.float32)
        block = jnp.exp2(score * POWER).astype(jnp.bfloat16)
        forward = jnp.dot(block, turned_ref[col_at], preferred_element_type=jnp.float32)
        mirror = jnp.dot(row_vecs_ref[row_at], block, preferred_element_type=jnp.float32)
        return slots_ref[2, slot], slots_ref[3, slot], forward, mirror

    @pl.loop(0, lax.div(count_ref[0, 0] + (UNROLL - 1), UNROLL))
    def _(group):
        done = [tile(group * UNROLL + step) for step in range(UNROLL)]
        for forward_at, mirror_at, forward, mirror in done:
            fsum_ref[forward_at] += forward
            msum_ref[mirror_at] += mirror

    @pl.loop(0, row_span)
    def _(block):
        turned = fsum_ref[block].T
        total = sum(turned[at * VECS : (at + 1) * VECS] for at in range(VEC_GROUP))
        forward_ref[block] = total.astype(jnp.bfloat16)

    mirror_ref[...] = msum_ref[0 : col_span // 2]
    mirror_other_ref[...] = msum_ref[col_span // 2 : col_span].astype(jnp.bfloat16)


def tile_products(slots, tile_count, row_parts, col_parts):
    row_span = sum(part.shape[0] for part in row_parts)
    col_span = sum(part.shape[0] for part in col_parts)
    smem = pl.BlockSpec(memory_space=pltpu.SMEM)
    vmem = pl.BlockSpec(memory_space=pltpu.VMEM)
    return pl.pallas_call(
        tiles_kernel,
        out_shape=(
            jax.ShapeDtypeStruct((row_span, VECS, TILE), jnp.bfloat16),
            jax.ShapeDtypeStruct((col_span // 2, VECS, TILE), jnp.float32),
            jax.ShapeDtypeStruct((col_span // 2, VECS, TILE), jnp.bfloat16),
        ),
        in_specs=[smem, smem] + [vmem] * (ROW_PARTS + COL_PARTS),
        out_specs=(vmem, vmem, vmem),
        scratch_shapes=[
            pltpu.VMEM((row_span, TILE, FULL), jnp.bfloat16),
            pltpu.VMEM((row_span, VECS, TILE), jnp.bfloat16),
            pltpu.VMEM((col_span, FULL, TILE), jnp.bfloat16),
            pltpu.VMEM((col_span, VECS, TILE), jnp.bfloat16),
            pltpu.VMEM((col_span, TILE, LANES), jnp.bfloat16),
            pltpu.VMEM((row_span + 1, TILE, LANES), jnp.float32),
            pltpu.VMEM((col_span + 1, VECS, TILE), jnp.float32),
        ],
        compiler_params=pltpu.CompilerParams(vmem_limit_bytes=36 * 1024 * 1024),
        name="tile_products",
    )(slots, tile_count, *row_parts, *col_parts)


def moved(value, axis, sizes, part, place_to):
    pairs = []
    for source in range(math.prod(sizes)):
        place = list(split_index(source, sizes))
        place[part] = place_to(place[part])
        target = 0
        for at, size in zip(place, sizes):
            target = target * size + at
        pairs.append((source, target))
    return lax.ppermute(value, axis, pairs)


def shifted(value, axis, sizes, part, distance):
    return moved(value, axis, sizes, part, lambda place: (place + distance) % sizes[part])


def swapped(value, axis, sizes, part, bit):
    return moved(value, axis, sizes, part, lambda place: place ^ bit)


def split_index(index, sizes):
    place = []
    for size in reversed(sizes):
        place.append(index & (size - 1))
        index = index >> (size.bit_length() - 1)
    return tuple(reversed(place))


def gather_rows(own):
    along_y = jnp.stack([own] + [shifted(own, "col", COL_SIZES, 0, step) for step in range(1, 4)])
    parts = [along_y] + [shifted(along_y, "col", COL_SIZES, 1, step) for step in range(1, 4)]
    return parts + [shifted(part, "col", COL_SIZES, 2, 1) for part in parts]


def grouped_all_to_all(value, axis, sizes, part_of):
    groups = {}
    for index in range(math.prod(sizes)):
        groups.setdefault(part_of(split_index(index, sizes)), []).append(index)
    return lax.all_to_all(value, axis, 0, 0, axis_index_groups=list(groups.values()), tiled=True)


def gather_cols(copies):
    along_z = grouped_all_to_all(copies, "row", ROW_SIZES, lambda place: place[0])
    return [along_z, swapped(along_z, "row", ROW_SIZES, 0, 1)]


def add_mirrors(mirror, for_neighbour):
    mirror = mirror + swapped(for_neighbour, "row", ROW_SIZES, 0, 1).astype(jnp.float32)
    sent = mirror.astype(jnp.bfloat16)
    received = [swapped(sent[bits : bits + 2], "row", ROW_SIZES, 1, bits) for bits in (2, 4, 6)]
    mirror = mirror[0:2] + sum(part.astype(jnp.float32) for part in received)
    return mirror[0] + swapped(mirror[1], "row", ROW_SIZES, 1, 1)


def slot_places(tile_pairs, tile_count):
    row_span = math.prod(COL_SIZES)
    col_span = math.prod(ROW_SIZES)
    i, j = tile_pairs[0], tile_pairs[1]
    local_row, local_col = lax.rem(i, row_span), lax.div(j, row_span)

    row_here, row_there = split_index(lax.axis_index("row"), ROW_SIZES), split_index(local_col, ROW_SIZES)
    col_here, col_there = split_index(lax.axis_index("col"), COL_SIZES), split_index(local_row, COL_SIZES)
    y_hi, x, core = [(mine - other) & (size - 1) for mine, other, size in zip(col_here, col_there, COL_SIZES)]
    live = jnp.arange(tile_pairs.shape[1], dtype=jnp.int32) < tile_count
    return jnp.stack(
        [
            (core * 4 + x) * 4 + y_hi,
            (row_there[0] ^ row_here[0]) * (col_span // 2) + row_there[1],
            jnp.where(live, local_row, row_span),
            jnp.where(live & (i != j), local_col ^ lax.axis_index("row"), col_span),
        ]
    )


def body(features, scales, vectors, pattern, counts):
    row_own, col_copies = pack_blocks(features, scales, vectors)
    col_parts = gather_cols(col_copies)
    row_parts = gather_rows(row_own)
    slots = slot_places(pattern[0, 0], counts[0, 0])
    forward, mirror, for_neighbour = tile_products(slots, counts, row_parts, col_parts)
    mirror = add_mirrors(mirror, for_neighbour)
    forward = lax.all_to_all(forward, "col", 0, 0, tiled=True)
    return jnp.sum(forward.astype(jnp.float32), axis=0) + mirror


def solution(mesh):
    placed = (
        P(("row", "col"), None),
        P(("row", "col")),
        P(None, ("row", "col")),
        P("row", "col", None, None),
        P("row", "col"),
    )
    return jax.shard_map(
        body, mesh=mesh, in_specs=placed, out_specs=P(None, ("row", "col")), check_vma=False
    )
```

```python
import math

import jax
import jax.numpy as jnp
from jax import lax
from jax.experimental import pallas as pl
from jax.experimental.pallas import tpu as pltpu
from jax.sharding import PartitionSpec as P

TILE = 256
DESC = 128
VECS = 32
AUG = 16
DEPTH = DESC + AUG
PACK = DEPTH + VECS
FULL = 256
LANES = 128
AUG_GROUP = LANES // AUG
VEC_GROUP = LANES // VECS
UNROLL = 8

COL_SIZES = (4, 4, 2)
ROW_SIZES = (2, 8)
ROW_PARTS = 8
COL_PARTS = 2

POWER = math.log2(math.e) * 2.0 / DESC


def pack_kernel(feat_ref, scale_ref, vec_ref, row_ref, col_ref):
    turned = feat_ref[...].astype(jnp.float32).T
    norm = jnp.sum(turned * turned, axis=0, keepdims=True)
    offset = (DESC // 2) * jnp.log(scale_ref[...].astype(jnp.float32).reshape(1, TILE)) - 0.5 * norm
    high = offset.astype(jnp.bfloat16).astype(jnp.float32)
    rest = offset - high
    middle = rest.astype(jnp.bfloat16).astype(jnp.float32)
    low = (rest - middle).astype(jnp.bfloat16).astype(jnp.float32)
    place = lax.broadcasted_iota(jnp.int32, (AUG, TILE), 0)

    def offset_rows(first_own, first_one):
        own = place - first_own
        rows = jnp.where(own == 0, high, jnp.where(own == 1, middle, jnp.where(own == 2, low, 0.0)))
        one = place - first_one
        return jnp.where((one >= 0) & (one < 3), 1.0, rows).astype(jnp.bfloat16)

    descriptors = turned.astype(jnp.bfloat16)
    narrow = vec_ref[...].astype(jnp.bfloat16)
    row_offsets, col_offsets = offset_rows(0, 3), offset_rows(3, 0)
    row_ref[0:DESC, 0:DESC] = feat_ref[0:DESC, :]
    row_ref[0:DESC, DESC:TILE] = feat_ref[DESC:TILE, :]
    row_ref[DESC:DEPTH, :] = row_offsets
    row_ref[DEPTH:PACK, :] = narrow
    for copy in range(col_ref.shape[0]):
        col_ref[copy, 0:DESC, :] = descriptors
        col_ref[copy, DESC:DEPTH, :] = col_offsets
        col_ref[copy, DEPTH:PACK, :] = narrow


def pack_blocks(features, scales, vectors):
    shapes = (
        jax.ShapeDtypeStruct((PACK, TILE), jnp.bfloat16),
        jax.ShapeDtypeStruct((ROW_SIZES[1], PACK, TILE), jnp.bfloat16),
    )
    return pl.pallas_call(pack_kernel, out_shape=shapes, name="pack_blocks")(
        features, scales, vectors
    )


def tiles_kernel(slots_ref, count_ref, *refs):
    rows_from, cols_from = refs[:ROW_PARTS], refs[ROW_PARTS : ROW_PARTS + COL_PARTS]
    forward_ref, mirror_ref, mirror_other_ref = refs[ROW_PARTS + COL_PARTS :][:3]
    left_ref, row_vecs_ref, right_ref, col_vecs_ref, turned_ref, fsum_ref, msum_ref = refs[ROW_PARTS + COL_PARTS + 3 :]
    row_span = left_ref.shape[0]
    col_span = right_ref.shape[0]

    fsum_ref[...] = jnp.zeros_like(fsum_ref)
    msum_ref[...] = jnp.zeros_like(msum_ref)
    lane = lax.broadcasted_iota(jnp.int32, (TILE, LANES), 1)

    def lanes_of(group, width):
        return jnp.where(lax.div(lane, width) == group, 1.0, 0.0).astype(jnp.bfloat16)

    offset_rows = []
    for at, part in enumerate(rows_from):
        size = part.shape[0]
        for own in range(size):
            block = at * size + own
            left_ref[block, 0:DESC, 0:DESC] = part[own, 0:DESC, 0:DESC]
            left_ref[block, DESC:TILE, 0:DESC] = part[own, 0:DESC, DESC:TILE]
            row_vecs_ref[block] = part[own, DEPTH:PACK, :]
            offset_rows.append(part[own, DESC:DEPTH, :])
            if len(offset_rows) == AUG_GROUP:
                turned = jnp.concatenate(offset_rows, axis=0).T
                for place in range(AUG_GROUP):
                    left_ref[block - AUG_GROUP + 1 + place, :, DESC:FULL] = turned * lanes_of(place, AUG)
                offset_rows = []

    for at, part in enumerate(cols_from):
        size = part.shape[0]

        @pl.loop(0, size)
        def _(own):
            right_ref[at * size + own, 0:DESC, :] = part[own, 0:DESC, :]
            offsets = part[own, DESC:DEPTH, :]
            for place in range(AUG_GROUP):
                right_ref[at * size + own, DESC + place * AUG : DESC + (place + 1) * AUG, :] = offsets
            col_vecs_ref[at * size + own] = part[own, DEPTH:PACK, :]

    @pl.loop(0, col_span // VEC_GROUP)
    def _(group):
        narrow = col_vecs_ref[pl.ds(group * VEC_GROUP, VEC_GROUP)].reshape(LANES, TILE).T
        for at in range(VEC_GROUP):
            turned_ref[group * VEC_GROUP + at] = narrow * lanes_of(at, VECS)

    def scores(slot):
        left, right = left_ref[slots_ref[0, slot]], right_ref[slots_ref[1, slot]]
        return jnp.dot(left, right, preferred_element_type=jnp.float32)

    def products(slot, score):
        block = jnp.exp2(score * POWER).astype(jnp.bfloat16)
        forward = jnp.dot(block, turned_ref[slots_ref[1, slot]], preferred_element_type=jnp.float32)
        mirror = jnp.dot(row_vecs_ref[slots_ref[0, slot]], block, preferred_element_type=jnp.float32)
        return slots_ref[2, slot], slots_ref[3, slot], forward, mirror

    @pl.loop(0, lax.div(count_ref[0, 0] + (UNROLL - 1), UNROLL))
    def _(group):
        done = []
        score = scores(group * UNROLL)
        for step in range(UNROLL):
            slot = group * UNROLL + step
            following = scores(slot + 1) if step + 1 < UNROLL else None
            done.append(products(slot, score))
            score = following
        for forward_at, mirror_at, forward, mirror in done:
            fsum_ref[forward_at] += forward
            msum_ref[mirror_at] += mirror

    lane_group = lax.div(lane, VECS)

    @pl.loop(0, row_span // VEC_GROUP)
    def _(group):
        sums = [fsum_ref[group * VEC_GROUP + at] for at in range(VEC_GROUP)]
        merged = None
        for shift in range(VEC_GROUP):
            chosen = sums[shift]
            for at in range(1, VEC_GROUP):
                chosen = jnp.where(lane_group == at, sums[(at + shift) % VEC_GROUP], chosen)
            if shift:
                chosen = pltpu.roll(chosen, shift * VECS, 1)
            merged = chosen if merged is None else merged + chosen
        turned = merged.T.astype(jnp.bfloat16)
        for at in range(VEC_GROUP):
            forward_ref[group * VEC_GROUP + at] = turned[at * VECS : (at + 1) * VECS]

    mirror_ref[...] = msum_ref[0 : col_span // 2]
    mirror_other_ref[...] = msum_ref[col_span // 2 : col_span].astype(jnp.bfloat16)


def tile_products(slots, tile_count, row_parts, col_parts):
    row_span = sum(part.shape[0] for part in row_parts)
    col_span = sum(part.shape[0] for part in col_parts)
    smem = pl.BlockSpec(memory_space=pltpu.SMEM)
    vmem = pl.BlockSpec(memory_space=pltpu.VMEM)
    return pl.pallas_call(
        tiles_kernel,
        out_shape=(
            jax.ShapeDtypeStruct((row_span, VECS, TILE), jnp.bfloat16),
            jax.ShapeDtypeStruct((col_span // 2, VECS, TILE), jnp.float32),
            jax.ShapeDtypeStruct((col_span // 2, VECS, TILE), jnp.bfloat16),
        ),
        in_specs=[smem, smem] + [vmem] * (ROW_PARTS + COL_PARTS),
        out_specs=(vmem, vmem, vmem),
        scratch_shapes=[
            pltpu.VMEM((row_span, TILE, FULL), jnp.bfloat16),
            pltpu.VMEM((row_span, VECS, TILE), jnp.bfloat16),
            pltpu.VMEM((col_span, FULL, TILE), jnp.bfloat16),
            pltpu.VMEM((col_span, VECS, TILE), jnp.bfloat16),
            pltpu.VMEM((col_span, TILE, LANES), jnp.bfloat16),
            pltpu.VMEM((row_span + 1, TILE, LANES), jnp.float32),
            pltpu.VMEM((col_span + 1, VECS, TILE), jnp.float32),
        ],
        compiler_params=pltpu.CompilerParams(vmem_limit_bytes=36 * 1024 * 1024),
        name="tile_products",
    )(slots, tile_count, *row_parts, *col_parts)


def moved(value, axis, sizes, part, place_to):
    pairs = []
    for source in range(math.prod(sizes)):
        place = list(split_index(source, sizes))
        place[part] = place_to(place[part])
        target = 0
        for at, size in zip(place, sizes):
            target = target * size + at
        pairs.append((source, target))
    return lax.ppermute(value, axis, pairs)


def shifted(value, axis, sizes, part, distance):
    return moved(value, axis, sizes, part, lambda place: (place + distance) % sizes[part])


def swapped(value, axis, sizes, part, bit):
    return moved(value, axis, sizes, part, lambda place: place ^ bit)


def split_index(index, sizes):
    place = []
    for size in reversed(sizes):
        place.append(index & (size - 1))
        index = index >> (size.bit_length() - 1)
    return tuple(reversed(place))


def gather_rows(own):
    along_y = jnp.stack([own] + [shifted(own, "col", COL_SIZES, 0, step) for step in range(1, 4)])
    parts = [along_y] + [shifted(along_y, "col", COL_SIZES, 1, step) for step in range(1, 4)]
    return parts + [shifted(part, "col", COL_SIZES, 2, 1) for part in parts]


def grouped_all_to_all(value, axis, sizes, part_of):
    groups = {}
    for index in range(math.prod(sizes)):
        groups.setdefault(part_of(split_index(index, sizes)), []).append(index)
    return lax.all_to_all(value, axis, 0, 0, axis_index_groups=list(groups.values()), tiled=True)


def gather_cols(copies):
    along_z = grouped_all_to_all(copies, "row", ROW_SIZES, lambda place: place[0])
    return [along_z, swapped(along_z, "row", ROW_SIZES, 0, 1)]


def add_mirrors(mirror, for_neighbour):
    mirror = mirror + swapped(for_neighbour, "row", ROW_SIZES, 0, 1).astype(jnp.float32)
    sent = mirror.astype(jnp.bfloat16)
    received = [swapped(sent[bits : bits + 2], "row", ROW_SIZES, 1, bits) for bits in (2, 4, 6)]
    mirror = mirror[0:2] + sum(part.astype(jnp.float32) for part in received)
    return mirror[0] + swapped(mirror[1], "row", ROW_SIZES, 1, 1)


def slot_places(tile_pairs, tile_count):
    row_span = math.prod(COL_SIZES)
    col_span = math.prod(ROW_SIZES)
    i, j = tile_pairs[0], tile_pairs[1]
    local_row, local_col = lax.rem(i, row_span), lax.div(j, row_span)

    row_here, row_there = split_index(lax.axis_index("row"), ROW_SIZES), split_index(local_col, ROW_SIZES)
    col_here, col_there = split_index(lax.axis_index("col"), COL_SIZES), split_index(local_row, COL_SIZES)
    y_hi, x, core = [(mine - other) & (size - 1) for mine, other, size in zip(col_here, col_there, COL_SIZES)]
    live = jnp.arange(tile_pairs.shape[1], dtype=jnp.int32) < tile_count
    return jnp.stack(
        [
            (core * 4 + x) * 4 + y_hi,
            (row_there[0] ^ row_here[0]) * (col_span // 2) + row_there[1],
            jnp.where(live, local_row, row_span),
            jnp.where(live & (i != j), local_col ^ lax.axis_index("row"), col_span),
        ]
    )


def body(features, scales, vectors, pattern, counts):
    row_own, col_copies = pack_blocks(features, scales, vectors)
    col_parts = gather_cols(col_copies)
    row_parts = gather_rows(row_own)
    slots = slot_places(pattern[0, 0], counts[0, 0])
    forward, mirror, for_neighbour = tile_products(slots, counts, row_parts, col_parts)
    mirror = add_mirrors(mirror, for_neighbour)
    forward = lax.all_to_all(forward, "col", 0, 0, tiled=True)
    return jnp.sum(forward.astype(jnp.float32), axis=0) + mirror


def solution(mesh):
    placed = (
        P(("row", "col"), None),
        P(("row", "col")),
        P(None, ("row", "col")),
        P("row", "col", None, None),
        P("row", "col"),
    )
    return jax.shard_map(
        body, mesh=mesh, in_specs=placed, out_specs=P(None, ("row", "col")), check_vma=False
    )
```

```python
import math

import jax
import jax.numpy as jnp
from jax import lax
from jax.experimental import pallas as pl
from jax.experimental.pallas import tpu as pltpu
from jax.sharding import PartitionSpec as P

TILE = 256
DESC = 128
VECS = 32
AUG = 16
DEPTH = DESC + AUG
PACK = DEPTH + VECS
FULL = 256
LANES = 128
AUG_GROUP = LANES // AUG
VEC_GROUP = LANES // VECS
UNROLL = 8

COL_SIZES = (4, 4, 2)
ROW_SIZES = (2, 8)
ROW_PARTS = 8
COL_PARTS = 2

POWER = math.log2(math.e) * 2.0 / DESC


def pack_kernel(feat_ref, scale_ref, vec_ref, row_ref, col_ref):
    turned = feat_ref[...].astype(jnp.float32).T
    norm = jnp.sum(turned * turned, axis=0, keepdims=True)
    offset = (DESC // 2) * jnp.log(scale_ref[...].astype(jnp.float32).reshape(1, TILE)) - 0.5 * norm
    high = offset.astype(jnp.bfloat16).astype(jnp.float32)
    rest = offset - high
    middle = rest.astype(jnp.bfloat16).astype(jnp.float32)
    low = (rest - middle).astype(jnp.bfloat16).astype(jnp.float32)
    place = lax.broadcasted_iota(jnp.int32, (AUG, TILE), 0)

    def offset_rows(first_own, first_one):
        own = place - first_own
        rows = jnp.where(own == 0, high, jnp.where(own == 1, middle, jnp.where(own == 2, low, 0.0)))
        one = place - first_one
        return jnp.where((one >= 0) & (one < 3), 1.0, rows).astype(jnp.bfloat16)

    descriptors = turned.astype(jnp.bfloat16)
    narrow = vec_ref[...].astype(jnp.bfloat16)
    row_offsets, col_offsets = offset_rows(0, 3), offset_rows(3, 0)
    row_ref[0:DESC, 0:DESC] = feat_ref[0:DESC, :]
    row_ref[0:DESC, DESC:TILE] = feat_ref[DESC:TILE, :]
    row_ref[DESC:DEPTH, :] = row_offsets
    row_ref[DEPTH:PACK, :] = narrow
    for copy in range(col_ref.shape[0]):
        col_ref[copy, 0:DESC, :] = descriptors
        col_ref[copy, DESC:DEPTH, :] = col_offsets
        col_ref[copy, DEPTH:PACK, :] = narrow


def pack_blocks(features, scales, vectors):
    shapes = (
        jax.ShapeDtypeStruct((PACK, TILE), jnp.bfloat16),
        jax.ShapeDtypeStruct((ROW_SIZES[1], PACK, TILE), jnp.bfloat16),
    )
    return pl.pallas_call(pack_kernel, out_shape=shapes, name="pack_blocks")(
        features, scales, vectors
    )


def tiles_kernel(slots_ref, count_ref, *refs):
    rows_from, cols_from = refs[:ROW_PARTS], refs[ROW_PARTS : ROW_PARTS + COL_PARTS]
    forward_ref, mirror_ref, mirror_other_ref = refs[ROW_PARTS + COL_PARTS :][:3]
    left_ref, row_vecs_ref, right_ref, col_vecs_ref, turned_ref, fsum_ref, msum_ref = refs[ROW_PARTS + COL_PARTS + 3 :]
    row_span = left_ref.shape[0]
    col_span = right_ref.shape[0]

    fsum_ref[...] = jnp.zeros_like(fsum_ref)
    msum_ref[...] = jnp.zeros_like(msum_ref)
    lane = lax.broadcasted_iota(jnp.int32, (TILE, LANES), 1)

    def lanes_of(group, width):
        return jnp.where(lax.div(lane, width) == group, 1.0, 0.0).astype(jnp.bfloat16)

    offset_rows = []
    for at, part in enumerate(rows_from):
        size = part.shape[0]
        for own in range(size):
            block = at * size + own
            left_ref[block, 0:DESC, 0:DESC] = part[own, 0:DESC, 0:DESC]
            left_ref[block, DESC:TILE, 0:DESC] = part[own, 0:DESC, DESC:TILE]
            row_vecs_ref[block] = part[own, DEPTH:PACK, :]
            offset_rows.append(part[own, DESC:DEPTH, :])
            if len(offset_rows) == AUG_GROUP:
                turned = jnp.concatenate(offset_rows, axis=0).T
                for place in range(AUG_GROUP):
                    left_ref[block - AUG_GROUP + 1 + place, :, DESC:FULL] = turned * lanes_of(place, AUG)
                offset_rows = []

    for at, part in enumerate(cols_from):
        size = part.shape[0]

        @pl.loop(0, size)
        def _(own):
            right_ref[at * size + own, 0:DESC, :] = part[own, 0:DESC, :]
            offsets = part[own, DESC:DEPTH, :]
            for place in range(AUG_GROUP):
                right_ref[at * size + own, DESC + place * AUG : DESC + (place + 1) * AUG, :] = offsets
            col_vecs_ref[at * size + own] = part[own, DEPTH:PACK, :]

    @pl.loop(0, col_span // VEC_GROUP)
    def _(group):
        narrow = col_vecs_ref[pl.ds(group * VEC_GROUP, VEC_GROUP)].reshape(LANES, TILE).T
        for at in range(VEC_GROUP):
            turned_ref[group * VEC_GROUP + at] = narrow * lanes_of(at, VECS)

    def scores(slot):
        left, right = left_ref[slots_ref[0, slot]], right_ref[slots_ref[1, slot]]
        return jnp.dot(left, right, preferred_element_type=jnp.float32)

    def weights(score):
        return jnp.exp2(score * POWER).astype(jnp.bfloat16)

    def add_products(slot, block):
        forward = jnp.dot(block, turned_ref[slots_ref[1, slot]], preferred_element_type=jnp.float32)
        mirror = jnp.dot(row_vecs_ref[slots_ref[0, slot]], block, preferred_element_type=jnp.float32)
        fsum_ref[slots_ref[2, slot]] += forward
        msum_ref[slots_ref[3, slot]] += mirror

    @pl.loop(0, lax.div(count_ref[0, 0] + (UNROLL - 1), UNROLL))
    def _(group):
        first = group * UNROLL
        score, block = scores(first), None
        for step in range(1, UNROLL + 2):
            following = scores(first + step) if step < UNROLL else None
            ready = weights(score) if score is not None else None
            if block is not None:
                add_products(first + step - 2, block)
            score, block = following, ready

    lane_group = lax.div(lane, VECS)

    @pl.loop(0, row_span // VEC_GROUP)
    def _(group):
        sums = [fsum_ref[group * VEC_GROUP + at] for at in range(VEC_GROUP)]
        merged = None
        for shift in range(VEC_GROUP):
            chosen = sums[shift]
            for at in range(1, VEC_GROUP):
                chosen = jnp.where(lane_group == at, sums[(at + shift) % VEC_GROUP], chosen)
            if shift:
                chosen = pltpu.roll(chosen, shift * VECS, 1)
            merged = chosen if merged is None else merged + chosen
        turned = merged.T.astype(jnp.bfloat16)
        for at in range(VEC_GROUP):
            forward_ref[group * VEC_GROUP + at] = turned[at * VECS : (at + 1) * VECS]

    mirror_ref[...] = msum_ref[0 : col_span // 2]
    mirror_other_ref[...] = msum_ref[col_span // 2 : col_span].astype(jnp.bfloat16)


def tile_products(slots, tile_count, row_parts, col_parts):
    row_span = sum(part.shape[0] for part in row_parts)
    col_span = sum(part.shape[0] for part in col_parts)
    smem = pl.BlockSpec(memory_space=pltpu.SMEM)
    vmem = pl.BlockSpec(memory_space=pltpu.VMEM)
    return pl.pallas_call(
        tiles_kernel,
        out_shape=(
            jax.ShapeDtypeStruct((row_span, VECS, TILE), jnp.bfloat16),
            jax.ShapeDtypeStruct((col_span // 2, VECS, TILE), jnp.float32),
            jax.ShapeDtypeStruct((col_span // 2, VECS, TILE), jnp.bfloat16),
        ),
        in_specs=[smem, smem] + [vmem] * (ROW_PARTS + COL_PARTS),
        out_specs=(vmem, vmem, vmem),
        scratch_shapes=[
            pltpu.VMEM((row_span, TILE, FULL), jnp.bfloat16),
            pltpu.VMEM((row_span, VECS, TILE), jnp.bfloat16),
            pltpu.VMEM((col_span, FULL, TILE), jnp.bfloat16),
            pltpu.VMEM((col_span, VECS, TILE), jnp.bfloat16),
            pltpu.VMEM((col_span, TILE, LANES), jnp.bfloat16),
            pltpu.VMEM((row_span + 1, TILE, LANES), jnp.float32),
            pltpu.VMEM((col_span + 1, VECS, TILE), jnp.float32),
        ],
        compiler_params=pltpu.CompilerParams(vmem_limit_bytes=36 * 1024 * 1024),
        name="tile_products",
    )(slots, tile_count, *row_parts, *col_parts)


def moved(value, axis, sizes, part, place_to):
    pairs = []
    for source in range(math.prod(sizes)):
        place = list(split_index(source, sizes))
        place[part] = place_to(place[part])
        target = 0
        for at, size in zip(place, sizes):
            target = target * size + at
        pairs.append((source, target))
    return lax.ppermute(value, axis, pairs)


def shifted(value, axis, sizes, part, distance):
    return moved(value, axis, sizes, part, lambda place: (place + distance) % sizes[part])


def swapped(value, axis, sizes, part, bit):
    return moved(value, axis, sizes, part, lambda place: place ^ bit)


def split_index(index, sizes):
    place = []
    for size in reversed(sizes):
        place.append(index & (size - 1))
        index = index >> (size.bit_length() - 1)
    return tuple(reversed(place))


def gather_rows(own):
    along_y = jnp.stack([own] + [shifted(own, "col", COL_SIZES, 0, step) for step in range(1, 4)])
    parts = [along_y] + [shifted(along_y, "col", COL_SIZES, 1, step) for step in range(1, 4)]
    return parts + [shifted(part, "col", COL_SIZES, 2, 1) for part in parts]


def grouped_all_to_all(value, axis, sizes, part_of):
    groups = {}
    for index in range(math.prod(sizes)):
        groups.setdefault(part_of(split_index(index, sizes)), []).append(index)
    return lax.all_to_all(value, axis, 0, 0, axis_index_groups=list(groups.values()), tiled=True)


def gather_cols(copies):
    along_z = grouped_all_to_all(copies, "row", ROW_SIZES, lambda place: place[0])
    return [along_z, swapped(along_z, "row", ROW_SIZES, 0, 1)]


def add_mirrors(mirror, for_neighbour):
    mirror = mirror + swapped(for_neighbour, "row", ROW_SIZES, 0, 1).astype(jnp.float32)
    sent = mirror.astype(jnp.bfloat16)
    received = [swapped(sent[bits : bits + 2], "row", ROW_SIZES, 1, bits) for bits in (2, 4, 6)]
    mirror = mirror[0:2] + sum(part.astype(jnp.float32) for part in received)
    return mirror[0] + swapped(mirror[1], "row", ROW_SIZES, 1, 1)


def slot_places(tile_pairs, tile_count):
    row_span = math.prod(COL_SIZES)
    col_span = math.prod(ROW_SIZES)
    i, j = tile_pairs[0], tile_pairs[1]
    local_row, local_col = lax.rem(i, row_span), lax.div(j, row_span)

    row_here, row_there = split_index(lax.axis_index("row"), ROW_SIZES), split_index(local_col, ROW_SIZES)
    col_here, col_there = split_index(lax.axis_index("col"), COL_SIZES), split_index(local_row, COL_SIZES)
    y_hi, x, core = [(mine - other) & (size - 1) for mine, other, size in zip(col_here, col_there, COL_SIZES)]
    live = jnp.arange(tile_pairs.shape[1], dtype=jnp.int32) < tile_count
    return jnp.stack(
        [
            (core * 4 + x) * 4 + y_hi,
            (row_there[0] ^ row_here[0]) * (col_span // 2) + row_there[1],
            jnp.where(live, local_row, row_span),
            jnp.where(live & (i != j), local_col ^ lax.axis_index("row"), col_span),
        ]
    )


def body(features, scales, vectors, pattern, counts):
    row_own, col_copies = pack_blocks(features, scales, vectors)
    col_parts = gather_cols(col_copies)
    row_parts = gather_rows(row_own)
    slots = slot_places(pattern[0, 0], counts[0, 0])
    forward, mirror, for_neighbour = tile_products(slots, counts, row_parts, col_parts)
    mirror = add_mirrors(mirror, for_neighbour)
    forward = lax.all_to_all(forward, "col", 0, 0, tiled=True)
    return jnp.sum(forward.astype(jnp.float32), axis=0) + mirror


def solution(mesh):
    placed = (
        P(("row", "col"), None),
        P(("row", "col")),
        P(None, ("row", "col")),
        P("row", "col", None, None),
        P("row", "col"),
    )
    return jax.shard_map(
        body, mesh=mesh, in_specs=placed, out_specs=P(None, ("row", "col")), check_vma=False
    )
```
